256 devices in a mesh: row: 8 (over z_lo, core), col: 8 (over y, z_hi), depth: 4 (over x).
Axes of the slice: x: 4, y: 4, z: 8 (z_hi: 2, z_lo: 4; z = z_hi * 4 + z_lo), core: 2. Of those that a mesh axis runs over, the one named last changes fastest.
Arguments:
- blocks: bfloat16 [1024, 28, 64, 64], P(('row', 'col'), 'depth'), may hold values from -6 to 6
- columns: int32 [1024, 28], P(('row', 'col'), 'depth'), may hold values from 0 to 1023, as said below
- counts: int32 [1024], P(('row', 'col')), may hold values from 20 to 28
- aggregate: int32 [1024], P(('row', 'col')), may hold values from 0 to 3
- coarse_slot: int32 [1024, 28], P(('row', 'col'), 'depth'), may hold values from 0 to 27
- prolong: bfloat16 [1024, 64, 64], P(('row', 'col')), may hold values from -0.75 to 0.75
Outputs:
- coarse: float32 [256, 28, 64, 64], P(('row', 'col'), 'depth')
The draws below stay inside these ranges and needn't reach their ends.
Inputs may be any that keep to these rules, and one draw needn't show every extreme that they name: The fine block row columns[i, s] belongs to a block-row group whose grid position differs from that of row i by at most one along each grid dimension; groups are numbered first dimension slowest, 16 rows each.
All inputs are finite; a program needn't handle non-finite values.
Results may differ from the reference program's by a relative error of at most 0.0029.
Values may be sent and summed in bfloat16 or wider, within the bound.
No kernel may reach another device: no remote copies, remote signals or barrier semaphores. Data moves between devices by JAX's collectives and lax.ppermute only.
A program may use at most 64 MiB of HBM per device.

```python
import jax
import jax.numpy as jnp

B = 64
SLOTS = 28
SC = 28
RB = 16
NA = 4
GRID_ROWS = 8
GRID_COLS = 8
NB = 1024
NAG = 256


def draw_columns(key, part):
    key = jax.random.fold_in(key, 11)
    first, second, third = jax.random.split(key, 3)
    groups = jnp.arange(NB, dtype=jnp.int32) // RB
    home_r = groups // GRID_COLS
    home_c = groups % GRID_COLS
    step_r = jax.random.randint(first, (NB, SLOTS), -1, 2)
    step_c = jax.random.randint(second, (NB, SLOTS), -1, 2)
    grid_r = jnp.clip(home_r[:, None] + step_r, 0, GRID_ROWS - 1)
    grid_c = jnp.clip(home_c[:, None] + step_c, 0, GRID_COLS - 1)
    local = jax.random.randint(third, (NB, SLOTS), 0, RB)
    result = (grid_r * GRID_COLS + grid_c) * RB + local
    result = result.at[0, 0].set(0).at[NB - 1, SLOTS - 1].set(NB - 1)
    return result.astype(jnp.int32)


def draw_counts(key, part):
    key = jax.random.fold_in(key, 23)
    result = jax.random.randint(key, (NB,), 20, SLOTS + 1)
    result = result.at[0].set(SLOTS).at[1].set(20)
    return result.astype(jnp.int32)


def set_ends(entries, stream_key, smallest, largest):
    dims = entries.shape
    index_at = [jax.random.randint(jax.random.fold_in(stream_key, axis), (), 0, dims[axis]) for axis in range(len(dims))]
    entries = entries.at[tuple(index_at)].set(smallest)
    longest = dims.index(max(dims))
    index_at[longest] = (index_at[longest] + 1) % dims[longest]
    return entries.at[tuple(index_at)].set(largest)


def block_scale(stream_key, shape, shards, smallest, top_value):
    loudness = 1.0
    for position, blocks in shards:
        steps = jax.random.uniform(jax.random.fold_in(jax.random.fold_in(stream_key, 6), position), (blocks,), jnp.float32, smallest / len(shards), top_value / len(shards))
        loudness = loudness * jnp.repeat(jnp.exp(steps), shape[position] // blocks).reshape((-1,) + (1,) * (len(shape) - 1 - position))
    return loudness


def centred(rng, shape, scale, reach, cuts=(), kind=jnp.bfloat16):
    values = scale * jax.random.normal(rng, shape, jnp.float32)
    if cuts:
        values = values * block_scale(rng, shape, cuts, -0.22, 0.18)
    return jnp.clip(values, -reach, reach).astype(kind)


def setup_inputs(seed: int = 0) -> dict:
    key_of = jax.random.split(jax.random.key(seed), 7)
    return {
        "blocks": centred(key_of[0], (NB, SLOTS, B, B), 1.0, 6.0, ((0, 64), (1, 4))),
        "columns": draw_columns(jax.random.fold_in(key_of[6], 71), 0),
        "counts": draw_counts(jax.random.fold_in(key_of[6], 71), 0),
        "aggregate": set_ends(jax.random.randint(key_of[3], (NB,), 0, NA), jax.random.fold_in(key_of[3], 1), 0, NA - 1).astype(jnp.int32),
        "coarse_slot": set_ends(jax.random.randint(key_of[4], (NB, SLOTS), 0, SC), jax.random.fold_in(key_of[4], 1), 0, SC - 1).astype(jnp.int32),
        "prolong": centred(key_of[5], (NB, B, B), B ** -0.5, 0.75, ((0, 64),)),
    }


def reference(blocks, columns, counts, aggregate, coarse_slot, prolong):
    slot_ids = jnp.arange(SLOTS, dtype=jnp.int32)
    used = slot_ids[None, :] < counts[:, None]
    picked = jnp.take(prolong, columns.reshape(-1), axis=0).reshape(NB, SLOTS, B, B)
    product = jnp.einsum("rsij,rsjk->rsik", blocks.astype(jnp.float32), picked.astype(jnp.float32))
    product = jnp.where(used[:, :, None, None], product, 0.0).astype(jnp.bfloat16)
    term = jnp.einsum("rji,rsjk->rsik", prolong.astype(jnp.float32), product.astype(jnp.float32))
    owner = (jnp.arange(NB, dtype=jnp.int32) // RB) * NA + aggregate
    target = owner[:, None] * SC + coarse_slot
    summed = jax.ops.segment_sum(term.reshape(NB * SLOTS, B * B), target.reshape(-1), num_segments=NAG * SC)
    return summed.reshape(NAG, SC, B, B)
```

```python
import functools

import jax
import jax.numpy as jnp
from jax import lax
from jax.experimental import pallas as pl
from jax.experimental.pallas import tpu as pltpu
from jax.sharding import PartitionSpec as P

SC = 28
ALL = ("row", "col", "depth")
VMEM = pl.BlockSpec(memory_space=pltpu.VMEM)
SMEM = pl.BlockSpec(memory_space=pltpu.SMEM)


def fold(block):
    half = block.shape[0] // 2
    return jnp.concatenate([block[:half], block[half:]], axis=1)


def unfold(block):
    half = block.shape[1] // 2
    return jnp.concatenate([block[:, :half], block[:, half:]], axis=0)


def pack_kernel(prolong_ref, out_ref):
    for i in range(prolong_ref.shape[0]):
        out_ref[i] = fold(prolong_ref[i])


def main_kernel(cols_ref, counts_ref, agg_ref, slot_ref, blocks_ref, prolong_ref, low_ref, mid_ref, high_ref,
                own_ref, one_ref, two_ref, three_ref, halo, acc):
    rows, slots = blocks_ref.shape[:2]
    depth = lax.axis_index("depth")
    home_r, home_c = lax.axis_index("row"), lax.axis_index("col")
    acc[...] = jnp.zeros_like(acc)
    group = 3 * rows
    halo[pl.ds(0, group)] = low_ref[...]
    halo[pl.ds(group, group)] = mid_ref[...]
    halo[pl.ds(2 * group, group)] = high_ref[...]
    far_side = jnp.where(depth < 2, 1, -1)

    def row_step(i, carry):
        left = prolong_ref[i].T
        count, agg = counts_ref[i], agg_ref[i]
        for s in range(slots):
            j = cols_ref[s, i]
            owner = j // rows
            dr = owner // 8 - home_r + 1
            dc = owner % 8 - home_c
            side = jnp.where(dc == 0, 0, jnp.where(dc == far_side, 1, 2))
            near = unfold(halo[(dr * 3 + side) * rows + j % rows])
            product = jnp.dot(blocks_ref[i, s], near, preferred_element_type=jnp.float32)
            used = depth * slots + s < count
            product = jnp.where(used, product, 0.0).astype(jnp.bfloat16)
            term = jnp.dot(left, product, preferred_element_type=jnp.float32)
            acc[slot_ref[s, i] * 4 + agg] += fold(term)
        return carry

    lax.fori_loop(0, rows, row_step, 0)
    size = own_ref.shape[0]
    for out, step in ((own_ref, 0), (one_ref, 1), (two_ref, 2), (three_ref, 3)):
        at = lax.rem(depth + step, 4) * size
        out[...] = acc[pl.ds(at, size)].astype(out.dtype)


def sum_kernel(own_ref, one_ref, two_ref, three_ref, out_ref):
    aggs, slots = out_ref.shape[:2]
    for a in range(aggs):
        for s in range(slots):
            at = s * aggs + a
            total = own_ref[at] + (
                one_ref[at].astype(jnp.float32) + two_ref[at].astype(jnp.float32) + three_ref[at].astype(jnp.float32)
            )
            out_ref[a, s] = unfold(total)


def per_device(blocks, columns, counts, aggregate, coarse_slot, prolong):
    rows, slots, width, _ = blocks.shape
    n_row, n_col, n_depth = (lax.axis_size(a) for a in ALL)

    def flat(r, c, d):
        return (r * n_col + c) * n_depth + d

    packed = pl.pallas_call(
        pack_kernel,
        out_shape=jax.ShapeDtypeStruct((rows, width // 2, 2 * width), prolong.dtype),
        in_specs=[VMEM],
        out_specs=VMEM,
        name="pack",
    )(prolong)
    far_perm = []
    for r in range(n_row):
        for c in range(n_col):
            for d in range(n_depth):
                source = c + 1 if d < n_depth // 2 else c - 1
                if 0 <= source < n_col:
                    far_perm.append((flat(r, source, d), flat(r, c, d)))
    far = lax.ppermute(packed, ALL, far_perm)
    other = lax.ppermute(far, "depth", [(d, n_depth - 1 - d) for d in range(n_depth)])
    mid = jnp.concatenate([packed, far, other], axis=0)
    up = [(r, r + 1) for r in range(n_row - 1)]
    low = lax.ppermute(mid, "row", up)
    high = lax.ppermute(mid, "row", [(b, a) for a, b in up])
    chunk = (SC // n_depth * 4, width // 2, 2 * width)
    own, one, two, three = pl.pallas_call(
        main_kernel,
        out_shape=[jax.ShapeDtypeStruct(chunk, jnp.float32)] + [jax.ShapeDtypeStruct(chunk, jnp.bfloat16)] * 3,
        in_specs=[SMEM] * 4 + [VMEM] * 5,
        out_specs=[VMEM] * 4,
        scratch_shapes=[
            pltpu.VMEM((9 * rows, width // 2, 2 * width), jnp.bfloat16),
            pltpu.VMEM((SC * 4, width // 2, 2 * width), jnp.float32),
        ],
        compiler_params=pltpu.CompilerParams(vmem_limit_bytes=40 * 2**20),
        name="galerkin",
    )(columns.T, counts, aggregate, coarse_slot.T, blocks, prolong, low, mid, high)
    got = [
        lax.ppermute(part, "depth", [(d, (d + k) % n_depth) for d in range(n_depth)])
        for k, part in ((1, one), (2, two), (3, three))
    ]
    return pl.pallas_call(
        sum_kernel,
        out_shape=jax.ShapeDtypeStruct((4, SC // n_depth, width, width), jnp.float32),
        in_specs=[VMEM] * 4,
        out_specs=VMEM,
        name="total",
    )(own, *got)


def solution(mesh):
    in_specs = (
        P(("row", "col"), "depth", None, None),
        P(("row", "col"), "depth"),
        P(("row", "col")),
        P(("row", "col")),
        P(("row", "col"), "depth"),
        P(("row", "col"), None, None),
    )
    out_specs = P(("row", "col"), "depth", None, None)
    return jax.shard_map(per_device, mesh=mesh, in_specs=in_specs, out_specs=out_specs, check_vma=False)
```

```python
import jax
import jax.numpy as jnp
from jax import lax
from jax.experimental import pallas as pl
from jax.experimental.pallas import tpu as pltpu
from jax.sharding import PartitionSpec as P

SC = 28
ALL = ("row", "col", "depth")
HBM = pl.BlockSpec(memory_space=pltpu.HBM)
VMEM = pl.BlockSpec(memory_space=pltpu.VMEM)
SMEM = pl.BlockSpec(memory_space=pltpu.SMEM)
LIMIT = pltpu.CompilerParams(vmem_limit_bytes=16 * 2**20)
BATCH = 56


def fold(block):
    half = block.shape[0] // 2
    return jnp.concatenate([block[:half], block[half:]], axis=1)


def unfold(block):
    half = block.shape[1] // 2
    return jnp.concatenate([block[:, :half], block[:, half:]], axis=0)


def pack_kernel(prolong_ref, out_ref):
    for i in range(prolong_ref.shape[0]):
        out_ref[i] = fold(prolong_ref[i])


def prep_kernel(cols_hbm, counts_hbm, agg_hbm, slot_hbm, blocks_hbm, packed_ref, blocks_ref, turned_ref, table_ref,
                cols_ref, counts_ref, agg_ref, slot_ref, sems):
    pairs = ((cols_hbm, cols_ref), (counts_hbm, counts_ref), (agg_hbm, agg_ref), (slot_hbm, slot_ref), (blocks_hbm, blocks_ref))
    copies = [pltpu.make_async_copy(a, b, sems.at[n]) for n, (a, b) in enumerate(pairs)]
    for copy in copies:
        copy.start()
    slots, rows = cols_ref.shape
    depth = lax.axis_index("depth")
    home_r, home_c = lax.axis_index("row"), lax.axis_index("col")
    across, flip = 1 - 2 * (home_c & 1), 1 - 2 * (home_r & 1)
    for i in range(rows):
        turned_ref[i] = unfold(packed_ref[i]).T
    for copy in copies[:4]:
        copy.wait()

    def row_step(i, carry):
        count, agg = counts_ref[i], agg_ref[i]
        for s in range(slots):
            j = cols_ref[s, i]
            dr = ((j >> 7) - home_r) * flip + 1
            dc = ((j >> 4) & 7) - home_c
            side = jnp.where(dc == 0, 0, jnp.where(dc == across, 1, 2))
            near = (dr * 3 + side) * rows + (j & 15)
            used = depth * slots + s < count
            target = jnp.where(used, slot_ref[s, i] * 4 + agg, SC * 4)
            table_ref[i * slots + s] = (near << 8) + target
        return carry

    lax.fori_loop(0, rows, row_step, 0)
    copies[4].wait()


def main_kernel(table_ref, blocks_ref, turned_ref, own_p, low_p, high_p, far_ref, other_ref, low_ref, high_ref,
                own_ref, one_ref, two_ref, three_ref, halo, acc):
    depth = lax.axis_index("depth")
    rows = own_p.shape[0]
    slots = blocks_ref.shape[0] // rows
    for at, part in enumerate((low_p, low_ref, own_p, far_ref, other_ref, high_p, high_ref)):
        first = (0, 1, 3, 4, 5, 6, 7)[at] * rows
        halo[pl.ds(first, part.shape[0])] = part[...]
    acc[...] = jnp.zeros_like(acc)

    for start in range(0, rows * slots, BATCH):
        items = range(start, start + BATCH)
        entries = [table_ref[n] for n in items]
        products = [
            jnp.dot(blocks_ref[n], unfold(halo[e >> 8]), preferred_element_type=jnp.float32).astype(jnp.bfloat16)
            for n, e in zip(items, entries)
        ]
        for n, e, product in zip(items, entries, products):
            term = jnp.dot(turned_ref[n // slots], product, preferred_element_type=jnp.float32)
            acc[e & 255] += fold(term)
    size = own_ref.shape[0]
    for out, step in ((own_ref, 0), (one_ref, 1), (two_ref, 2), (three_ref, 3)):
        at = lax.rem(depth + step, 4) * size
        out[...] = acc[pl.ds(at, size)].astype(out.dtype)


def sum_kernel(own_ref, one_ref, two_ref, three_ref, out_hbm, total_ref, sems):
    aggs, slots = total_ref.shape[:2]
    copies = []
    for a in range(aggs):
        for s in range(slots):
            at = s * aggs + a
            total = own_ref[at] + (
                one_ref[at].astype(jnp.float32) + two_ref[at].astype(jnp.float32) + three_ref[at].astype(jnp.float32)
            )
            total_ref[a, s] = unfold(total)
        copies.append(pltpu.make_async_copy(total_ref.at[a], out_hbm.at[a], sems.at[a]))
        copies[-1].start()
    for copy in copies:
        copy.wait()


def per_device(blocks, columns, counts, aggregate, coarse_slot, prolong):
    rows, slots, width, _ = blocks.shape
    n_row, n_col, n_depth = (lax.axis_size(a) for a in ALL)
    piece = (width // 2, 2 * width)

    packed = pl.pallas_call(
        pack_kernel,
        out_shape=jax.ShapeDtypeStruct((rows, *piece), prolong.dtype),
        in_specs=[VMEM],
        out_specs=VMEM,
        compiler_params=LIMIT,
        name="pack",
    )(prolong)
    far = lax.ppermute(packed, "col", [(c, c ^ 1) for c in range(n_col)])
    block_vmem, turned, table = pl.pallas_call(
        prep_kernel,
        out_shape=[
            jax.ShapeDtypeStruct((rows * slots, width, width), blocks.dtype),
            jax.ShapeDtypeStruct((rows, width, width), prolong.dtype),
            jax.ShapeDtypeStruct((rows * slots,), jnp.int32),
        ],
        in_specs=[HBM] * 5 + [VMEM],
        out_specs=[VMEM, VMEM, SMEM],
        scratch_shapes=[
            pltpu.SMEM((slots, rows), jnp.int32),
            pltpu.SMEM((rows,), jnp.int32),
            pltpu.SMEM((rows,), jnp.int32),
            pltpu.SMEM((slots, rows), jnp.int32),
            pltpu.SemaphoreType.DMA((5,)),
        ],
        compiler_params=LIMIT,
        cost_estimate=pl.CostEstimate(flops=0, bytes_accessed=4 * 2**20, transcendentals=0),
        name="prep",
    )(columns.T, counts, aggregate, coarse_slot.T, blocks.reshape(rows * slots, width, width), packed)

    core = [(r, r ^ 1) for r in range(n_row)]
    chip = [(r, r - 1) for r in range(2, n_row, 2)] + [(r, r + 1) for r in range(1, n_row - 1, 2)]

    def row_exchange(part):
        same, next_ = lax.ppermute(part, "row", core), lax.ppermute(part, "row", chip)
        even = lax.axis_index("row") % 2 == 0
        return same, next_, even

    far, packed_late, turned = lax.optimization_barrier((far, packed, turned))
    p_core, p_chip, _ = row_exchange(packed_late)
    fetch = [(c - 2, c) for c in range(2, n_col, 2)] + [(c + 2, c) for c in range(1, n_col - 2, 2)]
    other = lax.ppermute(far, "col", fetch)
    both = jnp.concatenate([far, other], axis=0)
    b_core, b_chip, even = row_exchange(both)
    chunk = (SC // n_depth * 4, *piece)

    own, one, two, three = pl.pallas_call(
        main_kernel,
        out_shape=[jax.ShapeDtypeStruct(chunk, jnp.float32)] + [jax.ShapeDtypeStruct(chunk, jnp.bfloat16)] * 3,
        in_specs=[SMEM] + [VMEM] * 9,
        out_specs=[VMEM] * 4,
        scratch_shapes=[
            pltpu.VMEM((9 * rows, *piece), jnp.bfloat16),
            pltpu.VMEM((SC * 4 + 1, *piece), jnp.float32),
        ],
        compiler_params=LIMIT,
        name="galerkin",
    )(table, block_vmem, turned, packed, p_chip, p_core, far, other, b_chip, b_core)
    got = {
        k: lax.ppermute(part, "depth", [(d, (d + k) % n_depth) for d in range(n_depth)])
        for k, part in ((2, two), (1, one), (3, three))
    }
    return pl.pallas_call(
        sum_kernel,
        out_shape=jax.ShapeDtypeStruct((4, SC // n_depth, width, width), jnp.float32),
        in_specs=[VMEM] * 4,
        out_specs=HBM,
        scratch_shapes=[
            pltpu.VMEM((4, SC // n_depth, width, width), jnp.float32),
            pltpu.SemaphoreType.DMA((4,)),
        ],
        compiler_params=LIMIT,
        name="total",
    )(own, got[1], got[2], got[3])


def solution(mesh):
    in_specs = (
        P(("row", "col"), "depth", None, None),
        P(("row", "col"), "depth"),
        P(("row", "col")),
        P(("row", "col")),
        P(("row", "col"), "depth"),
        P(("row", "col"), None, None),
    )
    out_specs = P(("row", "col"), "depth", None, None)
    return jax.shard_map(per_device, mesh=mesh, in_specs=in_specs, out_specs=out_specs, check_vma=False)
```

```python
import jax
import jax.numpy as jnp
from jax import lax
from jax.experimental import pallas as pl
from jax.experimental.pallas import tpu as pltpu
from jax.sharding import PartitionSpec as P

SC = 28
PART = 7
ALL = ("row", "col", "depth")
HBM = pl.BlockSpec(memory_space=pltpu.HBM)
VMEM = pl.BlockSpec(memory_space=pltpu.VMEM)
SMEM = pl.BlockSpec(memory_space=pltpu.SMEM)
LIMIT = pltpu.CompilerParams(vmem_limit_bytes=16 * 2**20)
BATCH = 40
SMALL = pl.CostEstimate(flops=1000, bytes_accessed=1000, transcendentals=0)
LIST = 288
CUTS = 4
MOVED = 8
SEND, OWN = range(2)
TRASH = 2 * SC


def fold(block):
    half = block.shape[0] // 2
    return jnp.concatenate([block[:half], block[half:]], axis=1)


def unfold(block):
    half = block.shape[1] // 2
    return jnp.concatenate([block[:, :half], block[:, half:]], axis=0)


def pack_kernel(prolong_ref, ints_ref, out_ref):
    for i in range(prolong_ref.shape[0]):
        out_ref[i] = fold(prolong_ref[i])


def blocks_kernel(blocks_hbm, packed_ref, ints_ref, first_ref, second_ref, turned_ref, blocks_ref, sems):
    half = first_ref.shape[0] - 1
    size = 2 * half // CUTS
    copies = [
        pltpu.make_async_copy(blocks_hbm.at[pl.ds(c * size, size)], blocks_ref.at[pl.ds(c * size, size)], sems.at[c])
        for c in range(CUTS)
    ]
    for copy in copies:
        copy.start()
    ints = ints_ref[...]
    coded = jnp.concatenate([ints >> 4, ints & 15], axis=0).astype(jnp.float32).astype(first_ref.dtype)
    for out in (first_ref, second_ref):
        out[half] = jnp.zeros(out.shape[1:], out.dtype)
        out[half, :, 0 : ints.shape[1]] = coded
    for i in range(packed_ref.shape[0]):
        turned_ref[i] = unfold(packed_ref[i]).T
    for c, copy in enumerate(copies):
        copy.wait()
        for n in range(c * size, (c + 1) * size):
            if n < half:
                first_ref[n] = fold(blocks_ref[n])
            else:
                second_ref[n - half] = fold(blocks_ref[n])


def entries_of(ints, depth, source, rel_b, row_ok, shift):
    count, agg = ints[2 * PART : 2 * PART + 1], ints[2 * PART + 1 : 2 * PART + 2]
    j, k = ints[:PART], ints[PART : 2 * PART]
    i = lax.broadcasted_iota(jnp.int32, j.shape, 1)
    s = lax.broadcasted_iota(jnp.int32, j.shape, 0)
    home_r, home_c = lax.axis_index("row"), lax.axis_index("col")
    across, flip = 1 - 2 * (home_c & 1), 1 - 2 * (home_r & 1)
    dest = (k * 37) >> 8
    rel = (dest - depth) & 3
    valid = ((rel == 0) | (rel == rel_b)) & (source * PART + s < count) & row_ok
    target = (jnp.where(rel == 3, PART, 0) + k - dest * PART) * 4 + agg
    dr = ((j >> 7) - home_r) * flip
    dc = ((j >> 4) & 7) - home_c
    side = jnp.where(dc == 0, 0, jnp.where(dc == across, 1, 2))
    place = side + 3 * jnp.where(dr == 0, 0, (dr + 3) >> 1)
    entry = (((((i << 8) + shift + i * PART + s) << 8) + place * 16 + (j & 15)) << 8) + target
    kind = jnp.where(rel == 0, OWN, SEND)
    return entry + jnp.where(valid, 1 << (28 + kind), 0)


def decoded(piece, rows):
    values = piece[:, :rows].astype(jnp.float32).astype(jnp.int32)
    return values[: values.shape[0] // 2] * 16 + values[values.shape[0] // 2 :]


def exact_dot(a, b):
    return jnp.dot(a.astype(jnp.bfloat16), b.astype(jnp.bfloat16), preferred_element_type=jnp.float32)


def make_lists(own_ref, prev_ref, next_ref, list_ref, sizes_ref, words_ref, places_ref, word_table, place_table, sems):
    rows = own_ref.shape[1]
    depth = lax.axis_index("depth")
    lane = lax.broadcasted_iota(jnp.int32, (PART, rows), 1)
    first = lane < rows // 2
    before, after = (depth + 3) & 3, (depth + 1) & 3
    own = entries_of(own_ref[...], depth, depth, jnp.where(first, 3, 1), lane >= 0, 0)
    from_prev = entries_of(decoded(prev_ref[prev_ref.shape[0] - 1], rows), depth, before, 1, first, rows * PART)
    from_next = entries_of(decoded(next_ref[next_ref.shape[0] - 1], rows), depth, after, 3, ~first, rows * PART)
    words_ref[...] = jnp.zeros_like(words_ref)
    words_ref[0:PART, 0:rows] = own
    words_ref[8 : 8 + PART, 0:rows] = jnp.where(first, from_prev, from_next)
    words = words_ref[...]
    lanes = words.shape[1]
    earlier = lax.broadcasted_iota(jnp.int32, (lanes, lanes), 0) < lax.broadcasted_iota(jnp.int32, (lanes, lanes), 1)
    above = lax.broadcasted_iota(jnp.int32, (16, 16), 0) > lax.broadcasted_iota(jnp.int32, (16, 16), 1)
    earlier, above = earlier.astype(jnp.float32), above.astype(jnp.float32)
    row = lax.broadcasted_iota(jnp.int32, words.shape, 0)
    places = jnp.full(words.shape, 2 * LIST, jnp.int32)
    for kind in range(2):
        here = (words >> (28 + kind)) & 1
        member = here.astype(jnp.float32)
        count = jnp.sum(member, axis=1, keepdims=True) + jnp.zeros_like(member)
        place = (exact_dot(member, earlier) + exact_dot(above, count)).astype(jnp.int32)
        total = jnp.sum(count, axis=0, keepdims=True).astype(jnp.int32)
        places = jnp.where(here == 1, place + kind * LIST, places)
        places = jnp.where(row == 7 + 8 * kind, total, places)
    places_ref[...] = places
    copies = [
        pltpu.make_async_copy(words_ref, word_table, sems.at[0]),
        pltpu.make_async_copy(places_ref, place_table, sems.at[1]),
    ]
    for copy in copies:
        copy.start()
    for copy in copies:
        copy.wait()

    def row_step(i, carry):
        for s in range(2 * PART):
            at = s + s // PART
            list_ref[place_table[at, i]] = word_table[at, i]
        return carry

    lax.fori_loop(0, rows, row_step, 0)
    for kind in range(2):
        size = place_table[7 + 8 * kind, 0]
        for p in range(BATCH):
            list_ref[kind * LIST + size + p] = TRASH
        sizes_ref[kind] = size


def run_list(list_ref, sizes_ref, kind, blocks_ref, turned_ref, halo_ref, acc_ref):
    def step(b, carry):
        entries = [list_ref[kind * LIST + b * BATCH + p] for p in range(BATCH)]
        products = [
            jnp.dot(
                unfold(blocks_ref[(e >> 16) & 255]), unfold(halo_ref[(e >> 8) & 255]), preferred_element_type=jnp.float32
            ).astype(jnp.bfloat16)
            for e in entries
        ]
        for e, product in zip(entries, products):
            term = jnp.dot(turned_ref[(e >> 24) & 15], product, preferred_element_type=jnp.float32)
            acc_ref[e & 255] += fold(term)
        return carry

    lax.fori_loop(0, lax.div(sizes_ref[kind] + (BATCH - 1), BATCH), step, 0)


def early_kernel(ints_ref, first_ref, second_ref, prev_ref, next_ref, packed_ref, far_ref, other_ref,
                 list_ref, sizes_ref, blocks_ref, halo_ref, words_ref, places_ref, word_table, place_table, sems):
    make_lists(ints_ref, prev_ref, next_ref, list_ref, sizes_ref, words_ref, places_ref, word_table, place_table, sems)
    half = first_ref.shape[0] - 1
    for at, part in enumerate((first_ref, second_ref, prev_ref, next_ref)):
        blocks_ref[pl.ds(at * half, half)] = part[0:half]
    rows = packed_ref.shape[0]
    for at, part in enumerate((packed_ref, far_ref, other_ref)):
        halo_ref[pl.ds(at * rows, part.shape[0])] = part[...]


def late_kernel(list_ref, sizes_ref, blocks_ref, turned_ref, chip_pair, core_pair, chip_ref, core_ref, halo_in,
                halo_ref, after_ref, before_ref, acc_ref):
    rows = halo_ref.shape[0] // 9
    for at, (one, two) in ((3, (chip_pair, chip_ref)), (6, (core_pair, core_ref))):
        halo_ref[pl.ds(at * rows, rows - MOVED)] = one[rows:]
        halo_ref[pl.ds((at + 1) * rows - MOVED, MOVED)] = two[rows:]
        halo_ref[pl.ds((at + 1) * rows, rows)] = one[0:rows]
        halo_ref[pl.ds((at + 2) * rows, rows)] = two[0:rows]
    acc_ref[...] = jnp.zeros_like(acc_ref)
    run_list(list_ref, sizes_ref, SEND, blocks_ref, turned_ref, halo_ref, acc_ref)
    after_ref[...] = acc_ref[0:SC].astype(after_ref.dtype)
    before_ref[...] = acc_ref[SC : 2 * SC].astype(before_ref.dtype)


def own_kernel(list_ref, sizes_ref, blocks_ref, turned_ref, halo_ref, acc_ref):
    acc_ref[...] = jnp.zeros_like(acc_ref)
    run_list(list_ref, sizes_ref, OWN, blocks_ref, turned_ref, halo_ref, acc_ref)


def sum_kernel(own_ref, one_ref, two_ref, out_hbm, total_ref, sems):
    aggs, slots = total_ref.shape[:2]
    copies = []
    for a in range(aggs):
        for s in range(slots):
            at = s * aggs + a
            total = own_ref[at] + (one_ref[at].astype(jnp.float32) + two_ref[at].astype(jnp.float32))
            total_ref[a, s] = unfold(total)
        copies.append(pltpu.make_async_copy(total_ref.at[a], out_hbm.at[a], sems.at[a]))
        copies[-1].start()
    for copy in copies:
        copy.wait()


def per_device(blocks, columns, counts, aggregate, coarse_slot, prolong):
    rows, slots, width, _ = blocks.shape
    n_row, n_col, n_depth = (lax.axis_size(a) for a in ALL)
    piece = (width // 2, 2 * width)
    bf16 = jnp.bfloat16
    tie = lax.optimization_barrier

    def struct(*shape, dtype=bf16):
        return jax.ShapeDtypeStruct(shape, dtype)

    ints = jnp.concatenate([columns.T, coarse_slot.T, counts[None], aggregate[None]], axis=0)
    packed = pl.pallas_call(
        pack_kernel, out_shape=struct(rows, *piece), in_specs=[VMEM, HBM], out_specs=VMEM, compiler_params=LIMIT, name="pack"
    )(prolong, ints)
    far = lax.ppermute(packed, "col", [(c, c ^ 1) for c in range(n_col)])

    half = rows * slots // 2
    first, second, turned = pl.pallas_call(
        blocks_kernel,
        out_shape=[struct(half + 1, *piece), struct(half + 1, *piece), struct(rows, width, width)],
        in_specs=[HBM, VMEM, VMEM],
        out_specs=[VMEM] * 3,
        scratch_shapes=[pltpu.VMEM((rows * slots, width, width), bf16), pltpu.SemaphoreType.DMA((CUTS,))],
        compiler_params=LIMIT,
        cost_estimate=SMALL,
        name="blocks",
    )(pltpu.with_memory_space_constraint(blocks.reshape(rows * slots, width, width), pltpu.HBM), packed, ints)
    up = [(d, (d + 1) % n_depth) for d in range(n_depth)]
    down = [(b, a) for a, b in up]
    from_prev, from_next = lax.ppermute(first, "depth", up), lax.ppermute(second, "depth", down)

    core = [(r, r ^ 1) for r in range(n_row)]
    chip = [(r, r - 1) for r in range(2, n_row, 2)] + [(r, r + 1) for r in range(1, n_row - 1, 2)]

    far, turned = tie((far, turned))
    fetch = [(c - 2, c) for c in range(2, n_col, 2)] + [(c + 2, c) for c in range(1, n_col - 2, 2)]
    other = lax.ppermute(far, "col", fetch)
    pair = jnp.concatenate([far, packed[: rows - MOVED]], axis=0)
    other_and = jnp.concatenate([other, packed[rows - MOVED :]], axis=0)
    chip_pair, core_pair = lax.ppermute(pair, "row", chip), lax.ppermute(pair, "row", core)
    chip_other, core_other = lax.ppermute(other_and, "row", chip), lax.ppermute(other_and, "row", core)

    sends = struct(TRASH + 1, *piece, dtype=jnp.float32)
    halos = struct(9 * rows, *piece)
    entries, sizes, all_blocks, halo = pl.pallas_call(
        early_kernel,
        out_shape=[
            struct(2 * LIST + 1, dtype=jnp.int32),
            struct(2, dtype=jnp.int32),
            struct(2 * rows * slots, *piece),
            halos,
        ],
        in_specs=[VMEM] * 8,
        out_specs=[SMEM] * 2 + [VMEM] * 2,
        scratch_shapes=[
            pltpu.VMEM((16, 128), jnp.int32),
            pltpu.VMEM((16, 128), jnp.int32),
            pltpu.SMEM((16, 128), jnp.int32),
            pltpu.SMEM((16, 128), jnp.int32),
            pltpu.SemaphoreType.DMA((2,)),
        ],
        compiler_params=LIMIT,
        name="early",
    )(ints, first, second, from_prev, from_next, packed, far, other)
    halo, after, before = pl.pallas_call(
        late_kernel,
        out_shape=[halos, struct(SC, *piece), struct(SC, *piece)],
        in_specs=[SMEM] * 2 + [VMEM] * 7,
        out_specs=[VMEM] * 3,
        scratch_shapes=[pltpu.VMEM((TRASH + 1, *piece), jnp.float32)],
        input_output_aliases={8: 0},
        compiler_params=LIMIT,
        name="late",
    )(entries, sizes, all_blocks, turned, chip_pair, core_pair, chip_other, core_other, halo)
    got_prev, got_next = lax.ppermute(after, "depth", up), lax.ppermute(before, "depth", down)
    own = pl.pallas_call(
        own_kernel,
        out_shape=sends,
        in_specs=[SMEM] * 2 + [VMEM] * 3,
        out_specs=VMEM,
        compiler_params=LIMIT,
        name="own",
    )(entries, sizes, all_blocks, turned, halo)
    return pl.pallas_call(
        sum_kernel,
        out_shape=struct(4, SC // n_depth, width, width, dtype=jnp.float32),
        in_specs=[VMEM] * 3,
        out_specs=HBM,
        scratch_shapes=[
            pltpu.VMEM((4, SC // n_depth, width, width), jnp.float32),
            pltpu.SemaphoreType.DMA((4,)),
        ],
        compiler_params=LIMIT,
        name="total",
    )(own, got_prev, got_next)


def solution(mesh):
    in_specs = (
        P(("row", "col"), "depth", None, None),
        P(("row", "col"), "depth"),
        P(("row", "col")),
        P(("row", "col")),
        P(("row", "col"), "depth"),
        P(("row", "col"), None, None),
    )
    out_specs = P(("row", "col"), "depth", None, None)
    return jax.shard_map(per_device, mesh=mesh, in_specs=in_specs, out_specs=out_specs, check_vma=False)
```

```python
import jax
import jax.numpy as jnp
from jax import lax
from jax.experimental import pallas as pl
from jax.experimental.pallas import tpu as pltpu
from jax.sharding import PartitionSpec as P

SC = 28
PART = 7
ALL = ("row", "col", "depth")
HBM = pl.BlockSpec(memory_space=pltpu.HBM)
VMEM = pl.BlockSpec(memory_space=pltpu.VMEM)
SMEM = pl.BlockSpec(memory_space=pltpu.SMEM)
LIMIT = pltpu.CompilerParams(vmem_limit_bytes=16 * 2**20)
BATCHES = (80, 40)
SMALL = pl.CostEstimate(flops=1000, bytes_accessed=1000, transcendentals=0)
LIST = 320
CUTS = 4
MOVED = 8
SEND, OWN = range(2)
TRASH = 2 * SC


def fold(block):
    half = block.shape[0] // 2
    return jnp.concatenate([block[:half], block[half:]], axis=1)


def unfold(block):
    half = block.shape[1] // 2
    return jnp.concatenate([block[:, :half], block[:, half:]], axis=0)


def pack_kernel(prolong_ref, out_ref):
    for i in range(prolong_ref.shape[0]):
        out_ref[i] = fold(prolong_ref[i])


def blocks_kernel(blocks_hbm, packed_ref, *refs):
    ints_hbm, (first_ref, second_ref, turned_ref, ints_ref), ints, (blocks_ref, sems) = refs[:4], refs[4:8], refs[8:12], refs[12:]
    half = first_ref.shape[0] - 1
    size = 2 * half // CUTS
    copies = [
        pltpu.make_async_copy(blocks_hbm.at[pl.ds(c * size, size)], blocks_ref.at[pl.ds(c * size, size)], sems.at[c])
        for c in range(CUTS)
    ]
    copies += [pltpu.make_async_copy(a, b, sems.at[CUTS + n]) for n, (a, b) in enumerate(zip(ints_hbm, ints))]
    for copy in copies:
        copy.start()
    for i in range(packed_ref.shape[0]):
        turned_ref[i] = unfold(packed_ref[i]).T
    for c in range(CUTS):
        copies[c].wait()
        for n in range(c * size, (c + 1) * size):
            if n < half:
                first_ref[n] = fold(blocks_ref[n])
            else:
                second_ref[n - half] = fold(blocks_ref[n])
    for copy in copies[CUTS:]:
        copy.wait()
    values = jnp.concatenate([ref[...] for ref in ints], axis=0)
    ints_ref[...] = values
    coded = jnp.concatenate([values >> 4, values & 15], axis=0).astype(jnp.float32).astype(first_ref.dtype)
    for out in (first_ref, second_ref):
        out[half] = jnp.zeros(out.shape[1:], out.dtype)
        out[half, :, 0 : values.shape[1]] = coded


def entries_of(ints, depth, source, rel_b, row_ok, shift):
    count, agg = ints[2 * PART : 2 * PART + 1], ints[2 * PART + 1 : 2 * PART + 2]
    j, k = ints[:PART], ints[PART : 2 * PART]
    i = lax.broadcasted_iota(jnp.int32, j.shape, 1)
    s = lax.broadcasted_iota(jnp.int32, j.shape, 0)
    home_r, home_c = lax.axis_index("row"), lax.axis_index("col")
    across, flip = 1 - 2 * (home_c & 1), 1 - 2 * (home_r & 1)
    dest = (k * 37) >> 8
    rel = (dest - depth) & 3
    valid = ((rel == 0) | (rel == rel_b)) & (source * PART + s < count) & row_ok
    target = (jnp.where(rel == 3, PART, 0) + k - dest * PART) * 4 + agg
    dr = ((j >> 7) - home_r) * flip
    dc = ((j >> 4) & 7) - home_c
    side = jnp.where(dc == 0, 0, jnp.where(dc == across, 1, 2))
    place = side + 3 * jnp.where(dr == 0, 0, (dr + 3) >> 1)
    entry = (((((i << 8) + shift + i * PART + s) << 8) + place * 16 + (j & 15)) << 8) + target
    kind = jnp.where(rel == 0, OWN, SEND)
    return entry + jnp.where(valid, 1 << (28 + kind), 0)


def decoded(piece, rows):
    values = piece[:, :rows].astype(jnp.float32).astype(jnp.int32)
    return values[: values.shape[0] // 2] * 16 + values[values.shape[0] // 2 :]


def exact_dot(a, b):
    return jnp.dot(a.astype(jnp.bfloat16), b.astype(jnp.bfloat16), preferred_element_type=jnp.float32)


def make_lists(own_ref, prev_ref, next_ref, list_ref, words_ref):
    rows = own_ref.shape[1]
    depth = lax.axis_index("depth")
    lane = lax.broadcasted_iota(jnp.int32, (PART, rows), 1)
    first = lane < rows // 2
    before, after = (depth + 3) & 3, (depth + 1) & 3
    own = entries_of(own_ref[...], depth, depth, jnp.where(first, 3, 1), lane >= 0, 0)
    from_prev = entries_of(decoded(prev_ref[prev_ref.shape[0] - 1], rows), depth, before, 1, first, rows * PART)
    from_next = entries_of(decoded(next_ref[next_ref.shape[0] - 1], rows), depth, after, 3, ~first, rows * PART)
    words_ref[...] = jnp.zeros_like(words_ref)
    words_ref[0:PART, 0:rows] = own
    words_ref[8 : 8 + PART, 0:rows] = jnp.where(first, from_prev, from_next)
    words = words_ref[...]
    lanes = words.shape[1]
    earlier = lax.broadcasted_iota(jnp.int32, (lanes, lanes), 0) < lax.broadcasted_iota(jnp.int32, (lanes, lanes), 1)
    above = lax.broadcasted_iota(jnp.int32, (16, 16), 0) > lax.broadcasted_iota(jnp.int32, (16, 16), 1)
    earlier, above = earlier.astype(jnp.float32), above.astype(jnp.float32)
    places = jnp.full(words.shape, 2.0 * LIST, jnp.float32)
    totals = []
    for kind in range(2):
        here = (words >> (28 + kind)) & 1
        member = here.astype(jnp.float32)
        count = jnp.sum(member, axis=1, keepdims=True) + jnp.zeros_like(member)
        place = exact_dot(member, earlier) + exact_dot(above, count)
        totals.append(jnp.sum(count, axis=0, keepdims=True)[:, 0:1].astype(jnp.int32))
        places = jnp.where(here == 1, place + kind * LIST, places)
    turned = places.T[0:rows]
    spot = lax.broadcasted_iota(jnp.int32, (rows, 2 * LIST), 1).astype(jnp.float32)
    fields = [TRASH - (words & 255), (words >> 8) & 255, (words >> 16) & 255, (words >> 24) & 15]
    fields = [f[:, 0:rows].astype(jnp.float32) for f in fields]
    blank = jnp.zeros((8 - len(fields), rows), jnp.float32)
    listed = jnp.zeros((8, 2 * LIST), jnp.float32)
    for r in (*range(PART), *range(8, 8 + PART)):
        chosen = jnp.where(turned[:, r : r + 1] == spot, 1.0, 0.0)
        listed = listed + exact_dot(jnp.concatenate([f[r : r + 1] for f in fields] + [blank], axis=0), chosen)
    target, place, block, row = (listed[n : n + 1].astype(jnp.int32) for n in range(4))
    entry = (((((row << 8) + block) << 8) + place) << 8) + TRASH - target
    spot = lax.broadcasted_iota(jnp.int32, entry.shape, 1)
    for kind in range(2):
        entry = jnp.where(spot == (kind + 1) * LIST - 1, totals[kind], entry)
    list_ref[...] = entry


def run_list(list_ref, kind, blocks_ref, turned_ref, halo_ref, acc_ref):
    batch = BATCHES[kind]

    def step(b, carry):
        entries = [list_ref[0, kind * LIST + b * batch + p] for p in range(batch)]
        products = [
            jnp.dot(
                unfold(blocks_ref[(e >> 16) & 255]), unfold(halo_ref[(e >> 8) & 255]), preferred_element_type=jnp.float32
            ).astype(jnp.bfloat16)
            for e in entries
        ]
        for e, product in zip(entries, products):
            term = jnp.dot(turned_ref[(e >> 24) & 15], product, preferred_element_type=jnp.float32)
            acc_ref[e & 255] += fold(term)
        return carry

    lax.fori_loop(0, lax.div(list_ref[0, (kind + 1) * LIST - 1] + (batch - 1), batch), step, 0)


def early_kernel(ints_ref, first_ref, second_ref, prev_ref, next_ref, packed_ref, far_ref, other_ref,
                 list_ref, blocks_ref, halo_ref, words_ref):
    make_lists(ints_ref, prev_ref, next_ref, list_ref, words_ref)
    half = first_ref.shape[0] - 1
    rows = packed_ref.shape[0]
    for at, part in enumerate((first_ref, second_ref, prev_ref, next_ref)):
        blocks_ref[pl.ds(at * half, half)] = part[0:half]
    for at, part in enumerate((packed_ref, far_ref, other_ref)):
        halo_ref[pl.ds(at * rows, part.shape[0])] = part[...]


def late_kernel(list_ref, blocks_ref, turned_ref, chip_pair, core_pair, chip_ref, core_ref, halo_in,
                halo_ref, after_ref, before_ref, acc_ref):
    rows = halo_ref.shape[0] // 9
    for at, (one, two) in ((3, (chip_pair, chip_ref)), (6, (core_pair, core_ref))):
        moved = two.shape[0] - rows
        halo_ref[pl.ds(at * rows, rows - moved)] = one[rows:]
        halo_ref[pl.ds((at + 1) * rows - moved, moved)] = two[rows:]
        halo_ref[pl.ds((at + 1) * rows, rows)] = one[0:rows]
        halo_ref[pl.ds((at + 2) * rows, rows)] = two[0:rows]
    acc_ref[...] = jnp.zeros_like(acc_ref)
    run_list(list_ref, SEND, blocks_ref, turned_ref, halo_ref, acc_ref)
    after_ref[...] = acc_ref[0:SC].astype(after_ref.dtype)
    before_ref[...] = acc_ref[SC : 2 * SC].astype(before_ref.dtype)


def own_kernel(list_ref, blocks_ref, turned_ref, halo_ref, acc_ref):
    acc_ref[...] = jnp.zeros_like(acc_ref)
    run_list(list_ref, OWN, blocks_ref, turned_ref, halo_ref, acc_ref)


def sum_kernel(own_ref, one_ref, two_ref, out_hbm, total_ref, sems):
    aggs, slots = total_ref.shape[:2]
    copies = []
    for a in range(aggs):
        for s in range(slots):
            at = s * aggs + a
            total = own_ref[at] + (one_ref[at].astype(jnp.float32) + two_ref[at].astype(jnp.float32))
            total_ref[a, s] = unfold(total)
        copies.append(pltpu.make_async_copy(total_ref.at[a], out_hbm.at[a], sems.at[a]))
        copies[-1].start()
    for copy in copies:
        copy.wait()


def per_device(blocks, columns, counts, aggregate, coarse_slot, prolong):
    rows, slots, width, _ = blocks.shape
    n_row, n_col, n_depth = (lax.axis_size(a) for a in ALL)
    piece = (width // 2, 2 * width)
    bf16 = jnp.bfloat16
    tie = lax.optimization_barrier

    def struct(*shape, dtype=bf16):
        return jax.ShapeDtypeStruct(shape, dtype)

    packed = pl.pallas_call(
        pack_kernel, out_shape=struct(rows, *piece), in_specs=[VMEM], out_specs=VMEM, compiler_params=LIMIT, name="pack"
    )(prolong)
    far = lax.ppermute(packed, "col", [(c, c ^ 1) for c in range(n_col)])

    half = rows * slots // 2
    blocks_hbm = pltpu.with_memory_space_constraint(blocks.reshape(rows * slots, width, width), pltpu.HBM)
    ints = [pltpu.with_memory_space_constraint(a, pltpu.HBM) for a in (columns.T, coarse_slot.T, counts[None], aggregate[None])]
    first, second, turned, ints = pl.pallas_call(
        blocks_kernel,
        out_shape=[
            struct(half + 1, *piece),
            struct(half + 1, *piece),
            struct(rows, width, width),
            struct(2 * slots + 2, rows, dtype=jnp.int32),
        ],
        in_specs=[HBM, VMEM] + [HBM] * 4,
        out_specs=[VMEM] * 4,
        scratch_shapes=[pltpu.VMEM(a.shape, a.dtype) for a in ints]
        + [pltpu.VMEM((rows * slots, width, width), bf16), pltpu.SemaphoreType.DMA((CUTS + 4,))],
        compiler_params=LIMIT,
        name="blocks",
    )(blocks_hbm, packed, *ints)
    up = [(d, (d + 1) % n_depth) for d in range(n_depth)]
    down = [(b, a) for a, b in up]
    from_prev, from_next = lax.ppermute(first, "depth", up), lax.ppermute(second, "depth", down)

    core = [(r, r ^ 1) for r in range(n_row)]
    chip = [(r, min(max(r - 1 + 2 * (r % 2), 0), n_row - 1)) for r in range(n_row)]

    far, turned = tie((far, turned))
    fetch = [((c - 2 + 4 * (c % 2)) % n_col, c) for c in range(n_col)]
    other = lax.ppermute(far, "col", fetch)
    pair = jnp.concatenate([far, packed[: rows - MOVED]], axis=0)
    other_and = jnp.concatenate([other, packed[rows - MOVED :]], axis=0)
    chip_pair, core_pair = lax.ppermute(pair, "row", chip), lax.ppermute(pair, "row", core)
    chip_other, core_other = lax.ppermute(other_and, "row", chip), lax.ppermute(other_and, "row", core)

    sends = struct(TRASH + 1, *piece, dtype=jnp.float32)
    halos = struct(9 * rows, *piece)
    entries, all_blocks, halo = pl.pallas_call(
        early_kernel,
        out_shape=[struct(1, 2 * LIST, dtype=jnp.int32), struct(2 * rows * slots, *piece), halos],
        in_specs=[VMEM] * 8,
        out_specs=[VMEM] * 3,
        scratch_shapes=[pltpu.VMEM((16, 128), jnp.int32)],
        compiler_params=LIMIT,
        name="early",
    )(ints, first, second, from_prev, from_next, packed, far, other)
    halo, after, before = pl.pallas_call(
        late_kernel,
        out_shape=[halos, struct(SC, *piece), struct(SC, *piece)],
        in_specs=[SMEM] + [VMEM] * 7,
        out_specs=[VMEM] * 3,
        scratch_shapes=[pltpu.VMEM((TRASH + 1, *piece), jnp.float32)],
        input_output_aliases={7: 0},
        compiler_params=LIMIT,
        name="late",
    )(entries, all_blocks, turned, chip_pair, core_pair, chip_other, core_other, halo)
    got_prev, got_next = lax.ppermute(after, "depth", up), lax.ppermute(before, "depth", down)
    own = pl.pallas_call(
        own_kernel,
        out_shape=sends,
        in_specs=[SMEM] + [VMEM] * 3,
        out_specs=VMEM,
        compiler_params=LIMIT,
        name="own",
    )(entries, all_blocks, turned, halo)
    return pl.pallas_call(
        sum_kernel,
        out_shape=struct(4, SC // n_depth, width, width, dtype=jnp.float32),
        in_specs=[VMEM] * 3,
        out_specs=HBM,
        scratch_shapes=[
            pltpu.VMEM((4, SC // n_depth, width, width), jnp.float32),
            pltpu.SemaphoreType.DMA((4,)),
        ],
        compiler_params=LIMIT,
        name="total",
    )(own, got_prev, got_next)


def solution(mesh):
    in_specs = (
        P(("row", "col"), "depth", None, None),
        P(("row", "col"), "depth"),
        P(("row", "col")),
        P(("row", "col")),
        P(("row", "col"), "depth"),
        P(("row", "col"), None, None),
    )
    out_specs = P(("row", "col"), "depth", None, None)
    return jax.shard_map(per_device, mesh=mesh, in_specs=in_specs, out_specs=out_specs, check_vma=False)
```

```python
import jax
import jax.numpy as jnp
from jax import lax
from jax.experimental import pallas as pl
from jax.experimental.pallas import tpu as pltpu
from jax.sharding import PartitionSpec as P

SC = 28
PART = 7
ALL = ("row", "col", "depth")
HBM = pl.BlockSpec(memory_space=pltpu.HBM)
VMEM = pl.BlockSpec(memory_space=pltpu.VMEM)
SMEM = pl.BlockSpec(memory_space=pltpu.SMEM)
LIMIT = pltpu.CompilerParams(vmem_limit_bytes=16 * 2**20)
BATCHES = (80, 40)
SMALL = pl.CostEstimate(flops=1000, bytes_accessed=1000, transcendentals=0)
LIST = 320
CUTS = 4
MOVED = 8
SEND, OWN = range(2)
TRASH = 2 * SC


def fold(block):
    half = block.shape[0] // 2
    return jnp.concatenate([block[:half], block[half:]], axis=1)


def unfold(block):
    half = block.shape[1] // 2
    return jnp.concatenate([block[:, :half], block[:, half:]], axis=0)


def pack_kernel(prolong_ref, out_ref):
    for i in range(prolong_ref.shape[0]):
        out_ref[i] = fold(prolong_ref[i])


def blocks_kernel(blocks_hbm, packed_ref, *refs):
    ints_hbm, (first_ref, second_ref, turned_ref, ints_ref), ints, (blocks_ref, sems) = refs[:4], refs[4:8], refs[8:12], refs[12:]
    half = first_ref.shape[0] - 1
    size = 2 * half // CUTS
    copies = [
        pltpu.make_async_copy(blocks_hbm.at[pl.ds(c * size, size)], blocks_ref.at[pl.ds(c * size, size)], sems.at[c])
        for c in range(CUTS)
    ]
    copies += [pltpu.make_async_copy(a, b, sems.at[CUTS + n]) for n, (a, b) in enumerate(zip(ints_hbm, ints))]
    for copy in copies:
        copy.start()
    for i in range(packed_ref.shape[0]):
        turned_ref[i] = unfold(packed_ref[i]).T
    for c in range(CUTS):
        copies[c].wait()
        for n in range(c * size, (c + 1) * size):
            if n < half:
                first_ref[n] = fold(blocks_ref[n])
            else:
                second_ref[n - half] = fold(blocks_ref[n])
    for copy in copies[CUTS:]:
        copy.wait()
    values = jnp.concatenate([ref[...] for ref in ints], axis=0)
    ints_ref[...] = values
    coded = jnp.concatenate([values >> 4, values & 15], axis=0).astype(jnp.float32).astype(first_ref.dtype)
    for out in (first_ref, second_ref):
        out[half] = jnp.zeros(out.shape[1:], out.dtype)
        out[half, :, 0 : values.shape[1]] = coded


def entries_of(ints, depth, source, rel_b, row_ok, shift):
    count, agg = ints[2 * PART : 2 * PART + 1], ints[2 * PART + 1 : 2 * PART + 2]
    j, k = ints[:PART], ints[PART : 2 * PART]
    i = lax.broadcasted_iota(jnp.int32, j.shape, 1)
    s = lax.broadcasted_iota(jnp.int32, j.shape, 0)
    home_r, home_c = lax.axis_index("row"), lax.axis_index("col")
    across, flip = 1 - 2 * (home_c & 1), 1 - 2 * (home_r & 1)
    dest = (k * 37) >> 8
    rel = (dest - depth) & 3
    valid = ((rel == 0) | (rel == rel_b)) & (source * PART + s < count) & row_ok
    target = (jnp.where(rel == 3, PART, 0) + k - dest * PART) * 4 + agg
    dr = ((j >> 7) - home_r) * flip
    dc = ((j >> 4) & 7) - home_c
    side = jnp.where(dc == 0, 0, jnp.where(dc == across, 1, 2))
    place = side + 3 * jnp.where(dr == 0, 0, (dr + 3) >> 1)
    entry = (((((i << 8) + shift + i * PART + s) << 8) + place * 16 + (j & 15)) << 8) + target
    kind = jnp.where(rel == 0, OWN, SEND)
    return entry + jnp.where(valid, 1 << (28 + kind), 0)


def decoded(piece, rows):
    values = piece[:, :rows].astype(jnp.float32).astype(jnp.int32)
    return values[: values.shape[0] // 2] * 16 + values[values.shape[0] // 2 :]


def exact_dot(a, b):
    return jnp.dot(a.astype(jnp.bfloat16), b.astype(jnp.bfloat16), preferred_element_type=jnp.float32)


def make_lists(own_ref, prev_ref, next_ref, list_ref, words_ref):
    rows = own_ref.shape[1]
    depth = lax.axis_index("depth")
    lane = lax.broadcasted_iota(jnp.int32, (PART, rows), 1)
    first = lane < rows // 2
    before, after = (depth + 3) & 3, (depth + 1) & 3
    own = entries_of(own_ref[...], depth, depth, jnp.where(first, 3, 1), lane >= 0, 0)
    from_prev = entries_of(decoded(prev_ref[prev_ref.shape[0] - 1], rows), depth, before, 1, first, rows * PART)
    from_next = entries_of(decoded(next_ref[next_ref.shape[0] - 1], rows), depth, after, 3, ~first, rows * PART)
    words_ref[...] = jnp.zeros_like(words_ref)
    words_ref[0:PART, 0:rows] = own
    words_ref[8 : 8 + PART, 0:rows] = jnp.where(first, from_prev, from_next)
    words = words_ref[...]
    lanes = words.shape[1]
    earlier = lax.broadcasted_iota(jnp.int32, (lanes, lanes), 0) < lax.broadcasted_iota(jnp.int32, (lanes, lanes), 1)
    above = lax.broadcasted_iota(jnp.int32, (16, 16), 0) > lax.broadcasted_iota(jnp.int32, (16, 16), 1)
    earlier, above = earlier.astype(jnp.float32), above.astype(jnp.float32)
    places = jnp.full(words.shape, 2.0 * LIST, jnp.float32)
    totals = []
    for kind in range(2):
        here = (words >> (28 + kind)) & 1
        member = here.astype(jnp.float32)
        count = jnp.sum(member, axis=1, keepdims=True) + jnp.zeros_like(member)
        place = exact_dot(member, earlier) + exact_dot(above, count)
        totals.append(jnp.sum(count, axis=0, keepdims=True)[:, 0:1].astype(jnp.int32))
        places = jnp.where(here == 1, place + kind * LIST, places)
    turned = places.T[0:rows]
    spot = lax.broadcasted_iota(jnp.int32, (rows, 2 * LIST), 1).astype(jnp.float32)
    fields = [TRASH - (words & 255), (words >> 8) & 255, (words >> 16) & 255, (words >> 24) & 15]
    fields = [f[:, 0:rows].astype(jnp.float32) for f in fields]
    blank = jnp.zeros((8 - len(fields), rows), jnp.float32)
    listed = jnp.zeros((8, 2 * LIST), jnp.float32)
    for r in (*range(PART), *range(8, 8 + PART)):
        chosen = jnp.where(turned[:, r : r + 1] == spot, 1.0, 0.0)
        listed = listed + exact_dot(jnp.concatenate([f[r : r + 1] for f in fields] + [blank], axis=0), chosen)
    target, place, block, row = (listed[n : n + 1].astype(jnp.int32) for n in range(4))
    entry = (((((row << 8) + block) << 8) + place) << 8) + TRASH - target
    spot = lax.broadcasted_iota(jnp.int32, entry.shape, 1)
    for kind in range(2):
        entry = jnp.where(spot == (kind + 1) * LIST - 1, totals[kind], entry)
    list_ref[...] = entry


def run_list(list_ref, kind, blocks_ref, turned_ref, halo_ref, acc_ref):
    batch = BATCHES[kind]

    def step(b, carry):
        entries = [list_ref[0, kind * LIST + b * batch + p] for p in range(batch)]
        products = [
            jnp.dot(
                unfold(blocks_ref[(e >> 16) & 255]), unfold(halo_ref[(e >> 8) & 255]), preferred_element_type=jnp.float32
            ).astype(jnp.bfloat16)
            for e in entries
        ]
        for e, product in zip(entries, products):
            term = jnp.dot(turned_ref[(e >> 24) & 15], product, preferred_element_type=jnp.float32)
            acc_ref[e & 255] += fold(term)
        return carry

    lax.fori_loop(0, lax.div(list_ref[0, (kind + 1) * LIST - 1] + (batch - 1), batch), step, 0)


def early_kernel(ints_ref, first_ref, second_ref, prev_ref, next_ref, packed_ref, far_ref, other_ref,
                 list_ref, blocks_ref, halo_ref, words_ref):
    make_lists(ints_ref, prev_ref, next_ref, list_ref, words_ref)
    half = first_ref.shape[0] - 1
    rows = packed_ref.shape[0]
    for at, part in enumerate((first_ref, second_ref, prev_ref, next_ref)):
        blocks_ref[pl.ds(at * half, half)] = part[0:half]
    for at, part in enumerate((packed_ref, far_ref, other_ref)):
        halo_ref[pl.ds(at * rows, part.shape[0])] = part[...]


def late_kernel(list_ref, blocks_ref, turned_ref, chip_pair, core_pair, chip_ref, core_ref, halo_in,
                halo_ref, after_ref, before_ref, acc_ref):
    rows = halo_ref.shape[0] // 9
    for at, (one, two) in ((3, (chip_pair, chip_ref)), (6, (core_pair, core_ref))):
        moved = two.shape[0] - rows
        halo_ref[pl.ds(at * rows, rows - moved)] = one[rows:]
        halo_ref[pl.ds((at + 1) * rows - moved, moved)] = two[rows:]
        halo_ref[pl.ds((at + 1) * rows, rows)] = one[0:rows]
        halo_ref[pl.ds((at + 2) * rows, rows)] = two[0:rows]
    acc_ref[...] = jnp.zeros_like(acc_ref)
    run_list(list_ref, SEND, blocks_ref, turned_ref, halo_ref, acc_ref)
    after_ref[...] = acc_ref[0:SC].astype(after_ref.dtype)
    before_ref[...] = acc_ref[SC : 2 * SC].astype(before_ref.dtype)


def own_kernel(list_ref, blocks_ref, turned_ref, halo_ref, acc_ref):
    acc_ref[...] = jnp.zeros_like(acc_ref)
    run_list(list_ref, OWN, blocks_ref, turned_ref, halo_ref, acc_ref)


def sum_kernel(own_ref, one_ref, two_ref, out_hbm, total_ref, sems):
    aggs, slots = total_ref.shape[:2]
    copies = []
    for a in range(aggs):
        for s in range(slots):
            at = s * aggs + a
            total = own_ref[at] + (one_ref[at].astype(jnp.float32) + two_ref[at].astype(jnp.float32))
            total_ref[a, s] = unfold(total)
        copies.append(pltpu.make_async_copy(total_ref.at[a], out_hbm.at[a], sems.at[a]))
        copies[-1].start()
    for copy in copies:
        copy.wait()


def per_device(blocks, columns, counts, aggregate, coarse_slot, prolong):
    rows, slots, width, _ = blocks.shape
    n_row, n_col, n_depth = (lax.axis_size(a) for a in ALL)
    piece = (width // 2, 2 * width)
    bf16 = jnp.bfloat16
    tie = lax.optimization_barrier

    def struct(*shape, dtype=bf16):
        return jax.ShapeDtypeStruct(shape, dtype)

    packed = pl.pallas_call(
        pack_kernel, out_shape=struct(rows, *piece), in_specs=[VMEM], out_specs=VMEM, compiler_params=LIMIT, name="pack"
    )(prolong)
    far = lax.ppermute(packed, "col", [(c, c ^ 1) for c in range(n_col)])

    half = rows * slots // 2
    blocks_hbm = pltpu.with_memory_space_constraint(blocks.reshape(rows * slots, width, width), pltpu.HBM)
    ints = [pltpu.with_memory_space_constraint(a, pltpu.HBM) for a in (columns.T, coarse_slot.T, counts[None], aggregate[None])]
    first, second, turned, ints = pl.pallas_call(
        blocks_kernel,
        out_shape=[
            struct(half + 1, *piece),
            struct(half + 1, *piece),
            struct(rows, width, width),
            struct(2 * slots + 2, rows, dtype=jnp.int32),
        ],
        in_specs=[HBM, VMEM] + [HBM] * 4,
        out_specs=[VMEM] * 4,
        scratch_shapes=[pltpu.VMEM(a.shape, a.dtype) for a in ints]
        + [pltpu.VMEM((rows * slots, width, width), bf16), pltpu.SemaphoreType.DMA((CUTS + 4,))],
        compiler_params=LIMIT,
        name="blocks",
    )(blocks_hbm, packed, *ints)
    up = [(d, (d + 1) % n_depth) for d in range(n_depth)]
    down = [(b, a) for a, b in up]
    from_prev, from_next = lax.ppermute(first, "depth", up), lax.ppermute(second, "depth", down)

    core = [(r, r ^ 1) for r in range(n_row)]
    chip = []
    for r in range(n_row):
        for c in range(n_col):
            step = r - 1 + 2 * (r % 2)
            inside = 0 <= step < n_row
            chip.append((r * n_col + c, (step % n_row) * n_col + (c if inside else c ^ 1)))

    far, turned = tie((far, turned))
    fetch = [((c - 2 + 4 * (c % 2)) % n_col, c) for c in range(n_col)]
    other = lax.ppermute(far, "col", fetch)
    pair = jnp.concatenate([far, packed[: rows - MOVED]], axis=0)
    other_and = jnp.concatenate([other, packed[rows - MOVED :]], axis=0)
    chip_pair, core_pair = lax.ppermute(pair, ("row", "col"), chip), lax.ppermute(pair, "row", core)
    chip_other, core_other = lax.ppermute(other_and, ("row", "col"), chip), lax.ppermute(other_and, "row", core)

    sends = struct(TRASH + 1, *piece, dtype=jnp.float32)
    halos = struct(9 * rows, *piece)
    entries, all_blocks, halo = pl.pallas_call(
        early_kernel,
        out_shape=[struct(1, 2 * LIST, dtype=jnp.int32), struct(2 * rows * slots, *piece), halos],
        in_specs=[VMEM] * 8,
        out_specs=[VMEM] * 3,
        scratch_shapes=[pltpu.VMEM((16, 128), jnp.int32)],
        compiler_params=LIMIT,
        name="early",
    )(ints, first, second, from_prev, from_next, packed, far, other)
    halo, after, before = pl.pallas_call(
        late_kernel,
        out_shape=[halos, struct(SC, *piece), struct(SC, *piece)],
        in_specs=[SMEM] + [VMEM] * 7,
        out_specs=[VMEM] * 3,
        scratch_shapes=[pltpu.VMEM((TRASH + 1, *piece), jnp.float32)],
        input_output_aliases={7: 0},
        compiler_params=LIMIT,
        name="late",
    )(entries, all_blocks, turned, chip_pair, core_pair, chip_other, core_other, halo)
    got_prev, got_next = lax.ppermute(after, "depth", up), lax.ppermute(before, "depth", down)
    own = pl.pallas_call(
        own_kernel,
        out_shape=sends,
        in_specs=[SMEM] + [VMEM] * 3,
        out_specs=VMEM,
        compiler_params=LIMIT,
        name="own",
    )(entries, all_blocks, turned, halo)
    return pl.pallas_call(
        sum_kernel,
        out_shape=struct(4, SC // n_depth, width, width, dtype=jnp.float32),
        in_specs=[VMEM] * 3,
        out_specs=HBM,
        scratch_shapes=[
            pltpu.VMEM((4, SC // n_depth, width, width), jnp.float32),
            pltpu.SemaphoreType.DMA((4,)),
        ],
        compiler_params=LIMIT,
        name="total",
    )(own, got_prev, got_next)


def solution(mesh):
    in_specs = (
        P(("row", "col"), "depth", None, None),
        P(("row", "col"), "depth"),
        P(("row", "col")),
        P(("row", "col")),
        P(("row", "col"), "depth"),
        P(("row", "col"), None, None),
    )
    out_specs = P(("row", "col"), "depth", None, None)
    return jax.shard_map(per_device, mesh=mesh, in_specs=in_specs, out_specs=out_specs, check_vma=False)
```

```python
import jax
import jax.numpy as jnp
from jax import lax
from jax.experimental import pallas as pl
from jax.experimental.pallas import tpu as pltpu
from jax.sharding import PartitionSpec as P

SC = 28
PART = 7
ALL = ("row", "col", "depth")
HBM = pl.BlockSpec(memory_space=pltpu.HBM)
VMEM = pl.BlockSpec(memory_space=pltpu.VMEM)
SMEM = pl.BlockSpec(memory_space=pltpu.SMEM)
LIMIT = pltpu.CompilerParams(vmem_limit_bytes=16 * 2**20)
BATCHES = (80, 40)
SMALL = pl.CostEstimate(flops=1000, bytes_accessed=1000, transcendentals=0)
LIST = 320
CUTS = 4
MOVED_CHIP = 2
MOVED_CORE = 9
SEND, OWN = range(2)
TRASH = 2 * SC


def fold(block):
    half = block.shape[0] // 2
    return jnp.concatenate([block[:half], block[half:]], axis=1)


def unfold(block):
    half = block.shape[1] // 2
    return jnp.concatenate([block[:, :half], block[:, half:]], axis=0)


def pack_kernel(prolong_ref, out_ref):
    for i in range(prolong_ref.shape[0]):
        out_ref[i] = fold(prolong_ref[i])


def blocks_kernel(blocks_hbm, packed_ref, *refs):
    ints_hbm, (first_ref, second_ref, turned_ref, ints_ref), ints, (blocks_ref, sems) = refs[:4], refs[4:8], refs[8:12], refs[12:]
    half = first_ref.shape[0] - 1
    size = 2 * half // CUTS
    copies = [
        pltpu.make_async_copy(blocks_hbm.at[pl.ds(c * size, size)], blocks_ref.at[pl.ds(c * size, size)], sems.at[c])
        for c in range(CUTS)
    ]
    copies += [pltpu.make_async_copy(a, b, sems.at[CUTS + n]) for n, (a, b) in enumerate(zip(ints_hbm, ints))]
    for copy in copies:
        copy.start()
    for i in range(packed_ref.shape[0]):
        turned_ref[i] = unfold(packed_ref[i]).T
    for c in range(CUTS):
        copies[c].wait()
        for n in range(c * size, (c + 1) * size):
            if n < half:
                first_ref[n] = fold(blocks_ref[n])
            else:
                second_ref[n - half] = fold(blocks_ref[n])
    for copy in copies[CUTS:]:
        copy.wait()
    values = jnp.concatenate([ref[...] for ref in ints], axis=0)
    ints_ref[...] = values
    coded = jnp.concatenate([values >> 4, values & 15], axis=0).astype(jnp.float32).astype(first_ref.dtype)
    for out in (first_ref, second_ref):
        out[half] = jnp.zeros(out.shape[1:], out.dtype)
        out[half, :, 0 : values.shape[1]] = coded


def entries_of(ints, depth, source, rel_b, row_ok, shift):
    count, agg = ints[2 * PART : 2 * PART + 1], ints[2 * PART + 1 : 2 * PART + 2]
    j, k = ints[:PART], ints[PART : 2 * PART]
    i = lax.broadcasted_iota(jnp.int32, j.shape, 1)
    s = lax.broadcasted_iota(jnp.int32, j.shape, 0)
    home_r, home_c = lax.axis_index("row"), lax.axis_index("col")
    across, flip = 1 - 2 * (home_c & 1), 1 - 2 * (home_r & 1)
    dest = (k * 37) >> 8
    rel = (dest - depth) & 3
    valid = ((rel == 0) | (rel == rel_b)) & (source * PART + s < count) & row_ok
    target = (jnp.where(rel == 3, PART, 0) + k - dest * PART) * 4 + agg
    dr = ((j >> 7) - home_r) * flip
    dc = ((j >> 4) & 7) - home_c
    side = jnp.where(dc == 0, 0, jnp.where(dc == across, 1, 2))
    place = side + 3 * jnp.where(dr == 0, 0, (dr + 3) >> 1)
    entry = (((((i << 8) + shift + i * PART + s) << 8) + place * 16 + (j & 15)) << 8) + target
    kind = jnp.where(rel == 0, OWN, SEND)
    return entry + jnp.where(valid, 1 << (28 + kind), 0)


def decoded(piece, rows):
    values = piece[:, :rows].astype(jnp.float32).astype(jnp.int32)
    return values[: values.shape[0] // 2] * 16 + values[values.shape[0] // 2 :]


def exact_dot(a, b):
    return jnp.dot(a.astype(jnp.bfloat16), b.astype(jnp.bfloat16), preferred_element_type=jnp.float32)


def make_lists(own_ref, prev_ref, next_ref, list_ref, words_ref):
    rows = own_ref.shape[1]
    depth = lax.axis_index("depth")
    lane = lax.broadcasted_iota(jnp.int32, (PART, rows), 1)
    first = lane < rows // 2
    before, after = (depth + 3) & 3, (depth + 1) & 3
    own = entries_of(own_ref[...], depth, depth, jnp.where(first, 3, 1), lane >= 0, 0)
    from_prev = entries_of(decoded(prev_ref[prev_ref.shape[0] - 1], rows), depth, before, 1, first, rows * PART)
    from_next = entries_of(decoded(next_ref[next_ref.shape[0] - 1], rows), depth, after, 3, ~first, rows * PART)
    words_ref[...] = jnp.zeros_like(words_ref)
    words_ref[0:PART, 0:rows] = own
    words_ref[8 : 8 + PART, 0:rows] = jnp.where(first, from_prev, from_next)
    words = words_ref[...]
    lanes = words.shape[1]
    earlier = lax.broadcasted_iota(jnp.int32, (lanes, lanes), 0) < lax.broadcasted_iota(jnp.int32, (lanes, lanes), 1)
    above = lax.broadcasted_iota(jnp.int32, (16, 16), 0) > lax.broadcasted_iota(jnp.int32, (16, 16), 1)
    earlier, above = earlier.astype(jnp.float32), above.astype(jnp.float32)
    places = jnp.full(words.shape, 2.0 * LIST, jnp.float32)
    totals = []
    for kind in range(2):
        here = (words >> (28 + kind)) & 1
        member = here.astype(jnp.float32)
        count = jnp.sum(member, axis=1, keepdims=True) + jnp.zeros_like(member)
        place = exact_dot(member, earlier) + exact_dot(above, count)
        totals.append(jnp.sum(count, axis=0, keepdims=True)[:, 0:1].astype(jnp.int32))
        places = jnp.where(here == 1, place + kind * LIST, places)
    turned = places.T[0:rows]
    spot = lax.broadcasted_iota(jnp.int32, (rows, 2 * LIST), 1).astype(jnp.float32)
    fields = [TRASH - (words & 255), (words >> 8) & 255, (words >> 16) & 255, (words >> 24) & 15]
    fields = [f[:, 0:rows].astype(jnp.float32) for f in fields]
    blank = jnp.zeros((8 - len(fields), rows), jnp.float32)
    listed = jnp.zeros((8, 2 * LIST), jnp.float32)
    for r in (*range(PART), *range(8, 8 + PART)):
        chosen = jnp.where(turned[:, r : r + 1] == spot, 1.0, 0.0)
        listed = listed + exact_dot(jnp.concatenate([f[r : r + 1] for f in fields] + [blank], axis=0), chosen)
    target, place, block, row = (listed[n : n + 1].astype(jnp.int32) for n in range(4))
    entry = (((((row << 8) + block) << 8) + place) << 8) + TRASH - target
    spot = lax.broadcasted_iota(jnp.int32, entry.shape, 1)
    for kind in range(2):
        entry = jnp.where(spot == (kind + 1) * LIST - 1, totals[kind], entry)
    list_ref[...] = entry


def run_list(list_ref, kind, blocks_ref, turned_ref, halo_ref, acc_ref):
    batch = BATCHES[kind]

    def step(b, carry):
        entries = [list_ref[0, kind * LIST + b * batch + p] for p in range(batch)]
        products = [
            jnp.dot(
                unfold(blocks_ref[(e >> 16) & 255]), unfold(halo_ref[(e >> 8) & 255]), preferred_element_type=jnp.float32
            ).astype(jnp.bfloat16)
            for e in entries
        ]
        for e, product in zip(entries, products):
            term = jnp.dot(turned_ref[(e >> 24) & 15], product, preferred_element_type=jnp.float32)
            acc_ref[e & 255] += fold(term)
        return carry

    lax.fori_loop(0, lax.div(list_ref[0, (kind + 1) * LIST - 1] + (batch - 1), batch), step, 0)


def early_kernel(ints_ref, first_ref, second_ref, prev_ref, next_ref, packed_ref, far_ref, other_ref,
                 list_ref, blocks_ref, halo_ref, words_ref):
    make_lists(ints_ref, prev_ref, next_ref, list_ref, words_ref)
    half = first_ref.shape[0] - 1
    rows = packed_ref.shape[0]
    for at, part in enumerate((first_ref, second_ref, prev_ref, next_ref)):
        blocks_ref[pl.ds(at * half, half)] = part[0:half]
    for at, part in enumerate((packed_ref, far_ref, other_ref)):
        halo_ref[pl.ds(at * rows, part.shape[0])] = part[...]


def late_kernel(list_ref, blocks_ref, turned_ref, chip_pair, core_pair, chip_ref, core_ref, halo_in,
                halo_ref, after_ref, before_ref, acc_ref):
    rows = halo_ref.shape[0] // 9
    for at, (one, two) in ((3, (chip_pair, chip_ref)), (6, (core_pair, core_ref))):
        moved = two.shape[0] - rows
        halo_ref[pl.ds(at * rows, rows - moved)] = one[rows:]
        halo_ref[pl.ds((at + 1) * rows - moved, moved)] = two[rows:]
        halo_ref[pl.ds((at + 1) * rows, rows)] = one[0:rows]
        halo_ref[pl.ds((at + 2) * rows, rows)] = two[0:rows]
    acc_ref[...] = jnp.zeros_like(acc_ref)
    run_list(list_ref, SEND, blocks_ref, turned_ref, halo_ref, acc_ref)
    after_ref[...] = acc_ref[0:SC].astype(after_ref.dtype)
    before_ref[...] = acc_ref[SC : 2 * SC].astype(before_ref.dtype)


def own_kernel(list_ref, blocks_ref, turned_ref, halo_ref, acc_ref):
    acc_ref[...] = jnp.zeros_like(acc_ref)
    run_list(list_ref, OWN, blocks_ref, turned_ref, halo_ref, acc_ref)


def sum_kernel(own_ref, one_ref, two_ref, out_hbm, total_ref, sems):
    aggs, slots = total_ref.shape[:2]
    copies = []
    for a in range(aggs):
        for s in range(slots):
            at = s * aggs + a
            total = own_ref[at] + (one_ref[at].astype(jnp.float32) + two_ref[at].astype(jnp.float32))
            total_ref[a, s] = unfold(total)
        copies.append(pltpu.make_async_copy(total_ref.at[a], out_hbm.at[a], sems.at[a]))
        copies[-1].start()
    for copy in copies:
        copy.wait()


def per_device(blocks, columns, counts, aggregate, coarse_slot, prolong):
    rows, slots, width, _ = blocks.shape
    n_row, n_col, n_depth = (lax.axis_size(a) for a in ALL)
    piece = (width // 2, 2 * width)
    bf16 = jnp.bfloat16
    tie = lax.optimization_barrier

    def struct(*shape, dtype=bf16):
        return jax.ShapeDtypeStruct(shape, dtype)

    packed = pl.pallas_call(
        pack_kernel, out_shape=struct(rows, *piece), in_specs=[VMEM], out_specs=VMEM, compiler_params=LIMIT, name="pack"
    )(prolong)
    far = lax.ppermute(packed, "col", [(c, c ^ 1) for c in range(n_col)])

    half = rows * slots // 2
    blocks_hbm = pltpu.with_memory_space_constraint(blocks.reshape(rows * slots, width, width), pltpu.HBM)
    ints = [pltpu.with_memory_space_constraint(a, pltpu.HBM) for a in (columns.T, coarse_slot.T, counts[None], aggregate[None])]
    first, second, turned, ints = pl.pallas_call(
        blocks_kernel,
        out_shape=[
            struct(half + 1, *piece),
            struct(half + 1, *piece),
            struct(rows, width, width),
            struct(2 * slots + 2, rows, dtype=jnp.int32),
        ],
        in_specs=[HBM, VMEM] + [HBM] * 4,
        out_specs=[VMEM] * 4,
        scratch_shapes=[pltpu.VMEM(a.shape, a.dtype) for a in ints]
        + [pltpu.VMEM((rows * slots, width, width), bf16), pltpu.SemaphoreType.DMA((CUTS + 4,))],
        compiler_params=LIMIT,
        name="blocks",
    )(blocks_hbm, packed, *ints)
    up = [(d, (d + 1) % n_depth) for d in range(n_depth)]
    down = [(b, a) for a, b in up]
    from_prev, from_next = lax.ppermute(first, "depth", up), lax.ppermute(second, "depth", down)

    core = [(r, r ^ 1) for r in range(n_row)]
    chip = []
    for r in range(n_row):
        for c in range(n_col):
            step = r - 1 + 2 * (r % 2)
            inside = 0 <= step < n_row
            chip.append((r * n_col + c, (step % n_row) * n_col + (c if inside else c ^ 1)))

    far, turned = tie((far, turned))
    fetch = [((c - 2 + 4 * (c % 2)) % n_col, c) for c in range(n_col)]
    other = lax.ppermute(far, "col", fetch)
    def cut(moved):
        pair = jnp.concatenate([far, packed[: rows - moved]], axis=0)
        return pair, jnp.concatenate([other, packed[rows - moved :]], axis=0)

    (chip_pair, chip_other), (core_pair, core_other) = (
        [lax.ppermute(part, axes, perm) for part in cut(moved)]
        for axes, perm, moved in ((("row", "col"), chip, MOVED_CHIP), ("row", core, MOVED_CORE))
    )

    sends = struct(TRASH + 1, *piece, dtype=jnp.float32)
    halos = struct(9 * rows, *piece)
    entries, all_blocks, halo = pl.pallas_call(
        early_kernel,
        out_shape=[struct(1, 2 * LIST, dtype=jnp.int32), struct(2 * rows * slots, *piece), halos],
        in_specs=[VMEM] * 8,
        out_specs=[VMEM] * 3,
        scratch_shapes=[pltpu.VMEM((16, 128), jnp.int32)],
        compiler_params=LIMIT,
        name="early",
    )(ints, first, second, from_prev, from_next, packed, far, other)
    halo, after, before = pl.pallas_call(
        late_kernel,
        out_shape=[halos, struct(SC, *piece), struct(SC, *piece)],
        in_specs=[SMEM] + [VMEM] * 7,
        out_specs=[VMEM] * 3,
        scratch_shapes=[pltpu.VMEM((TRASH + 1, *piece), jnp.float32)],
        input_output_aliases={7: 0},
        compiler_params=LIMIT,
        name="late",
    )(entries, all_blocks, turned, chip_pair, core_pair, chip_other, core_other, halo)
    got_prev, got_next = lax.ppermute(after, "depth", up), lax.ppermute(before, "depth", down)
    own = pl.pallas_call(
        own_kernel,
        out_shape=sends,
        in_specs=[SMEM] + [VMEM] * 3,
        out_specs=VMEM,
        compiler_params=LIMIT,
        name="own",
    )(entries, all_blocks, turned, halo)
    return pl.pallas_call(
        sum_kernel,
        out_shape=struct(4, SC // n_depth, width, width, dtype=jnp.float32),
        in_specs=[VMEM] * 3,
        out_specs=HBM,
        scratch_shapes=[
            pltpu.VMEM((4, SC // n_depth, width, width), jnp.float32),
            pltpu.SemaphoreType.DMA((4,)),
        ],
        compiler_params=LIMIT,
        name="total",
    )(own, got_prev, got_next)


def solution(mesh):
    in_specs = (
        P(("row", "col"), "depth", None, None),
        P(("row", "col"), "depth"),
        P(("row", "col")),
        P(("row", "col")),
        P(("row", "col"), "depth"),
        P(("row", "col"), None, None),
    )
    out_specs = P(("row", "col"), "depth", None, None)
    return jax.shard_map(per_device, mesh=mesh, in_specs=in_specs, out_specs=out_specs, check_vma=False)
```

```python
import jax
import jax.numpy as jnp
from jax import lax
from jax.experimental import pallas as pl
from jax.experimental.pallas import tpu as pltpu
from jax.sharding import PartitionSpec as P

SC = 28
PART = 7
ALL = ("row", "col", "depth")
HBM = pl.BlockSpec(memory_space=pltpu.HBM)
VMEM = pl.BlockSpec(memory_space=pltpu.VMEM)
SMEM = pl.BlockSpec(memory_space=pltpu.SMEM)
LIMIT = pltpu.CompilerParams(vmem_limit_bytes=16 * 2**20)
BATCHES = (80, 40)
SMALL = pl.CostEstimate(flops=1000, bytes_accessed=1000, transcendentals=0)
LIST = 320
CUTS = 4
MOVED = 8
SEND, OWN = range(2)
TRASH = 2 * SC


def fold(block):
    half = block.shape[0] // 2
    return jnp.concatenate([block[:half], block[half:]], axis=1)


def unfold(block):
    half = block.shape[1] // 2
    return jnp.concatenate([block[:, :half], block[:, half:]], axis=0)


def pack_kernel(prolong_hbm, out_ref, prolong_ref, sems):
    size = prolong_ref.shape[0] // 2
    copies = [
        pltpu.make_async_copy(prolong_hbm.at[pl.ds(c * size, size)], prolong_ref.at[pl.ds(c * size, size)], sems.at[c])
        for c in range(2)
    ]
    for copy in copies:
        copy.start()
    for c, copy in enumerate(copies):
        copy.wait()
        for i in range(c * size, (c + 1) * size):
            out_ref[i] = fold(prolong_ref[i])


def blocks_kernel(blocks_hbm, packed_ref, *refs):
    ints_hbm, (first_ref, second_ref, turned_ref, ints_ref), ints, (blocks_ref, sems) = refs[:4], refs[4:8], refs[8:12], refs[12:]
    half = first_ref.shape[0] - 1
    size = 2 * half // CUTS
    copies = [
        pltpu.make_async_copy(blocks_hbm.at[pl.ds(c * size, size)], blocks_ref.at[pl.ds(c * size, size)], sems.at[c])
        for c in range(CUTS)
    ]
    copies += [pltpu.make_async_copy(a, b, sems.at[CUTS + n]) for n, (a, b) in enumerate(zip(ints_hbm, ints))]
    for copy in copies:
        copy.start()
    for i in range(packed_ref.shape[0]):
        turned_ref[i] = unfold(packed_ref[i]).T
    for c in range(CUTS):
        copies[c].wait()
        for n in range(c * size, (c + 1) * size):
            if n < half:
                first_ref[n] = fold(blocks_ref[n])
            else:
                second_ref[n - half] = fold(blocks_ref[n])
    for copy in copies[CUTS:]:
        copy.wait()
    values = jnp.concatenate([ref[...] for ref in ints], axis=0)
    ints_ref[...] = values
    coded = jnp.concatenate([values >> 4, values & 15], axis=0).astype(jnp.float32).astype(first_ref.dtype)
    for out in (first_ref, second_ref):
        out[half] = jnp.zeros(out.shape[1:], out.dtype)
        out[half, :, 0 : values.shape[1]] = coded


def entries_of(ints, depth, source, rel_b, row_ok, shift):
    count, agg = ints[2 * PART : 2 * PART + 1], ints[2 * PART + 1 : 2 * PART + 2]
    j, k = ints[:PART], ints[PART : 2 * PART]
    i = lax.broadcasted_iota(jnp.int32, j.shape, 1)
    s = lax.broadcasted_iota(jnp.int32, j.shape, 0)
    home_r, home_c = lax.axis_index("row"), lax.axis_index("col")
    across, flip = 1 - 2 * (home_c & 1), 1 - 2 * (home_r & 1)
    dest = (k * 37) >> 8
    rel = (dest - depth) & 3
    valid = ((rel == 0) | (rel == rel_b)) & (source * PART + s < count) & row_ok
    target = (jnp.where(rel == 3, PART, 0) + k - dest * PART) * 4 + agg
    dr = ((j >> 7) - home_r) * flip
    dc = ((j >> 4) & 7) - home_c
    side = jnp.where(dc == 0, 0, jnp.where(dc == across, 1, 2))
    place = side + 3 * jnp.where(dr == 0, 0, (dr + 3) >> 1)
    entry = (((((i << 8) + shift + i * PART + s) << 8) + place * 16 + (j & 15)) << 8) + target
    kind = jnp.where(rel == 0, OWN, SEND)
    return entry + jnp.where(valid, 1 << (28 + kind), 0)


def decoded(piece, rows):
    values = piece[:, :rows].astype(jnp.float32).astype(jnp.int32)
    return values[: values.shape[0] // 2] * 16 + values[values.shape[0] // 2 :]


def exact_dot(a, b):
    return jnp.dot(a.astype(jnp.bfloat16), b.astype(jnp.bfloat16), preferred_element_type=jnp.float32)


def make_lists(own_ref, prev_ref, next_ref, list_ref, words_ref):
    rows = own_ref.shape[1]
    depth = lax.axis_index("depth")
    lane = lax.broadcasted_iota(jnp.int32, (PART, rows), 1)
    first = lane < rows // 2
    before, after = (depth + 3) & 3, (depth + 1) & 3
    own = entries_of(own_ref[...], depth, depth, jnp.where(first, 3, 1), lane >= 0, 0)
    from_prev = entries_of(decoded(prev_ref[prev_ref.shape[0] - 1], rows), depth, before, 1, first, rows * PART)
    from_next = entries_of(decoded(next_ref[next_ref.shape[0] - 1], rows), depth, after, 3, ~first, rows * PART)
    words_ref[...] = jnp.zeros_like(words_ref)
    words_ref[0:PART, 0:rows] = own
    words_ref[8 : 8 + PART, 0:rows] = jnp.where(first, from_prev, from_next)
    words = words_ref[...]
    lanes = words.shape[1]
    earlier = lax.broadcasted_iota(jnp.int32, (lanes, lanes), 0) < lax.broadcasted_iota(jnp.int32, (lanes, lanes), 1)
    above = lax.broadcasted_iota(jnp.int32, (16, 16), 0) > lax.broadcasted_iota(jnp.int32, (16, 16), 1)
    earlier, above = earlier.astype(jnp.float32), above.astype(jnp.float32)
    places = jnp.full(words.shape, 2.0 * LIST, jnp.float32)
    totals = []
    for kind in range(2):
        here = (words >> (28 + kind)) & 1
        member = here.astype(jnp.float32)
        count = jnp.sum(member, axis=1, keepdims=True) + jnp.zeros_like(member)
        place = exact_dot(member, earlier) + exact_dot(above, count)
        totals.append(jnp.sum(count, axis=0, keepdims=True)[:, 0:1].astype(jnp.int32))
        places = jnp.where(here == 1, place + kind * LIST, places)
    turned = places.T[0:rows]
    spot = lax.broadcasted_iota(jnp.int32, (rows, 2 * LIST), 1).astype(jnp.float32)
    fields = [TRASH - (words & 255), (words >> 8) & 255, (words >> 16) & 255, (words >> 24) & 15]
    fields = [f[:, 0:rows].astype(jnp.float32) for f in fields]
    blank = jnp.zeros((8 - len(fields), rows), jnp.float32)
    listed = jnp.zeros((8, 2 * LIST), jnp.float32)
    for r in (*range(PART), *range(8, 8 + PART)):
        chosen = jnp.where(turned[:, r : r + 1] == spot, 1.0, 0.0)
        listed = listed + exact_dot(jnp.concatenate([f[r : r + 1] for f in fields] + [blank], axis=0), chosen)
    target, place, block, row = (listed[n : n + 1].astype(jnp.int32) for n in range(4))
    entry = (((((row << 8) + block) << 8) + place) << 8) + TRASH - target
    spot = lax.broadcasted_iota(jnp.int32, entry.shape, 1)
    for kind in range(2):
        entry = jnp.where(spot == (kind + 1) * LIST - 1, totals[kind], entry)
    list_ref[...] = entry


def run_list(list_ref, kind, blocks_ref, turned_ref, halo_ref, acc_ref):
    batch = BATCHES[kind]

    def step(b, carry):
        entries = [list_ref[0, kind * LIST + b * batch + p] for p in range(batch)]
        products = [
            jnp.dot(
                unfold(blocks_ref[(e >> 16) & 255]), unfold(halo_ref[(e >> 8) & 255]), preferred_element_type=jnp.float32
            ).astype(jnp.bfloat16)
            for e in entries
        ]
        for e, product in zip(entries, products):
            term = jnp.dot(turned_ref[(e >> 24) & 15], product, preferred_element_type=jnp.float32)
            acc_ref[e & 255] += fold(term)
        return carry

    lax.fori_loop(0, lax.div(list_ref[0, (kind + 1) * LIST - 1] + (batch - 1), batch), step, 0)


def early_kernel(ints_ref, first_ref, second_ref, prev_ref, next_ref, packed_ref, far_ref, other_ref,
                 list_ref, blocks_ref, halo_ref, words_ref):
    make_lists(ints_ref, prev_ref, next_ref, list_ref, words_ref)
    half = first_ref.shape[0] - 1
    rows = packed_ref.shape[0]
    for at, part in enumerate((first_ref, second_ref, prev_ref, next_ref)):
        blocks_ref[pl.ds(at * half, half)] = part[0:half]
    for at, part in enumerate((packed_ref, far_ref, other_ref)):
        halo_ref[pl.ds(at * rows, part.shape[0])] = part[...]


def late_kernel(list_ref, blocks_ref, turned_ref, chip_pair, core_pair, chip_ref, core_ref, halo_in,
                halo_ref, after_ref, before_ref, acc_ref):
    rows = halo_ref.shape[0] // 9
    for at, (one, two) in ((3, (chip_pair, chip_ref)), (6, (core_pair, core_ref))):
        moved = two.shape[0] - rows
        halo_ref[pl.ds(at * rows, rows - moved)] = one[rows:]
        halo_ref[pl.ds((at + 1) * rows - moved, moved)] = two[rows:]
        halo_ref[pl.ds((at + 1) * rows, rows)] = one[0:rows]
        halo_ref[pl.ds((at + 2) * rows, rows)] = two[0:rows]
    acc_ref[...] = jnp.zeros_like(acc_ref)
    run_list(list_ref, SEND, blocks_ref, turned_ref, halo_ref, acc_ref)
    after_ref[...] = acc_ref[0:SC].astype(after_ref.dtype)
    before_ref[...] = acc_ref[SC : 2 * SC].astype(before_ref.dtype)


def own_kernel(list_ref, blocks_ref, turned_ref, halo_ref, acc_ref):
    acc_ref[...] = jnp.zeros_like(acc_ref)
    run_list(list_ref, OWN, blocks_ref, turned_ref, halo_ref, acc_ref)


def sum_kernel(own_ref, one_ref, two_ref, out_hbm, total_ref, sems):
    aggs, slots = total_ref.shape[:2]
    copies = []
    for a in range(aggs):
        for s in range(slots):
            at = s * aggs + a
            total = own_ref[at] + (one_ref[at].astype(jnp.float32) + two_ref[at].astype(jnp.float32))
            total_ref[a, s] = unfold(total)
        copies.append(pltpu.make_async_copy(total_ref.at[a], out_hbm.at[a], sems.at[a]))
        copies[-1].start()
    for copy in copies:
        copy.wait()


def per_device(blocks, columns, counts, aggregate, coarse_slot, prolong):
    rows, slots, width, _ = blocks.shape
    n_row, n_col, n_depth = (lax.axis_size(a) for a in ALL)
    piece = (width // 2, 2 * width)
    bf16 = jnp.bfloat16
    tie = lax.optimization_barrier

    def struct(*shape, dtype=bf16):
        return jax.ShapeDtypeStruct(shape, dtype)

    packed = pl.pallas_call(
        pack_kernel,
        out_shape=struct(rows, *piece),
        in_specs=[HBM],
        out_specs=VMEM,
        scratch_shapes=[pltpu.VMEM(prolong.shape, prolong.dtype), pltpu.SemaphoreType.DMA((2,))],
        compiler_params=LIMIT,
        name="pack",
    )(pltpu.with_memory_space_constraint(prolong, pltpu.HBM))
    far = lax.ppermute(packed, "col", [(c, c ^ 1) for c in range(n_col)])

    half = rows * slots // 2
    blocks_hbm = pltpu.with_memory_space_constraint(blocks.reshape(rows * slots, width, width), pltpu.HBM)
    ints = [pltpu.with_memory_space_constraint(a, pltpu.HBM) for a in (columns.T, coarse_slot.T, counts[None], aggregate[None])]
    first, second, turned, ints = pl.pallas_call(
        blocks_kernel,
        out_shape=[
            struct(half + 1, *piece),
            struct(half + 1, *piece),
            struct(rows, width, width),
            struct(2 * slots + 2, rows, dtype=jnp.int32),
        ],
        in_specs=[HBM, VMEM] + [HBM] * 4,
        out_specs=[VMEM] * 4,
        scratch_shapes=[pltpu.VMEM(a.shape, a.dtype) for a in ints]
        + [pltpu.VMEM((rows * slots, width, width), bf16), pltpu.SemaphoreType.DMA((CUTS + 4,))],
        compiler_params=LIMIT,
        name="blocks",
    )(blocks_hbm, packed, *ints)
    up = [(d, (d + 1) % n_depth) for d in range(n_depth)]
    down = [(b, a) for a, b in up]
    from_prev, from_next = lax.ppermute(first, "depth", up), lax.ppermute(second, "depth", down)

    core = [(r, r ^ 1) for r in range(n_row)]
    chip = []
    for r in range(n_row):
        for c in range(n_col):
            step = r - 1 + 2 * (r % 2)
            inside = 0 <= step < n_row
            chip.append((r * n_col + c, (step % n_row) * n_col + (c if inside else c ^ 1)))

    far, turned = tie((far, turned))
    fetch = [((c - 2 + 4 * (c % 2)) % n_col, c) for c in range(n_col)]
    other = lax.ppermute(far, "col", fetch)
    pair = jnp.concatenate([far, packed[: rows - MOVED]], axis=0)
    other_and = jnp.concatenate([other, packed[rows - MOVED :]], axis=0)
    chip_pair, core_pair = lax.ppermute(pair, ("row", "col"), chip), lax.ppermute(pair, "row", core)
    chip_other, core_other = lax.ppermute(other_and, ("row", "col"), chip), lax.ppermute(other_and, "row", core)

    sends = struct(TRASH + 1, *piece, dtype=jnp.float32)
    halos = struct(9 * rows, *piece)
    entries, all_blocks, halo = pl.pallas_call(
        early_kernel,
        out_shape=[struct(1, 2 * LIST, dtype=jnp.int32), struct(2 * rows * slots, *piece), halos],
        in_specs=[VMEM] * 8,
        out_specs=[VMEM] * 3,
        scratch_shapes=[pltpu.VMEM((16, 128), jnp.int32)],
        compiler_params=LIMIT,
        name="early",
    )(ints, first, second, from_prev, from_next, packed, far, other)
    halo, after, before = pl.pallas_call(
        late_kernel,
        out_shape=[halos, struct(SC, *piece), struct(SC, *piece)],
        in_specs=[SMEM] + [VMEM] * 7,
        out_specs=[VMEM] * 3,
        scratch_shapes=[pltpu.VMEM((TRASH + 1, *piece), jnp.float32)],
        input_output_aliases={7: 0},
        compiler_params=LIMIT,
        name="late",
    )(entries, all_blocks, turned, chip_pair, core_pair, chip_other, core_other, halo)
    got_prev, got_next = lax.ppermute(after, "depth", up), lax.ppermute(before, "depth", down)
    own = pl.pallas_call(
        own_kernel,
        out_shape=sends,
        in_specs=[SMEM] + [VMEM] * 3,
        out_specs=VMEM,
        compiler_params=LIMIT,
        name="own",
    )(entries, all_blocks, turned, halo)
    return pl.pallas_call(
        sum_kernel,
        out_shape=struct(4, SC // n_depth, width, width, dtype=jnp.float32),
        in_specs=[VMEM] * 3,
        out_specs=HBM,
        scratch_shapes=[
            pltpu.VMEM((4, SC // n_depth, width, width), jnp.float32),
            pltpu.SemaphoreType.DMA((4,)),
        ],
        compiler_params=LIMIT,
        name="total",
    )(own, got_prev, got_next)


def solution(mesh):
    in_specs = (
        P(("row", "col"), "depth", None, None),
        P(("row", "col"), "depth"),
        P(("row", "col")),
        P(("row", "col")),
        P(("row", "col"), "depth"),
        P(("row", "col"), None, None),
    )
    out_specs = P(("row", "col"), "depth", None, None)
    return jax.shard_map(per_device, mesh=mesh, in_specs=in_specs, out_specs=out_specs, check_vma=False)
```
